256 devices in a mesh: seq: 32 (over z, y), head: 8 (over x, core).
Axes of the slice: x: 4, y: 4, z: 8, core: 2. Of those that a mesh axis runs over, the one named last changes fastest.
Arguments:
- query: bfloat16 [49152, 3072], P(('seq', 'head')), may hold values from -40 to 40
- key: bfloat16 [49152, 3072], P(('seq', 'head')), may hold values from -4 to 4
- value: bfloat16 [49152, 3072], P(('seq', 'head')), may hold values from -6 to 6
- raster_to_tile: int32 [49152], P(('seq', 'head')), may hold values from 0 to 49151, as said below
- window_list: int32 [128, 4], P('seq'), may hold values from 0 to 127, as said below
- valid_count: int32 [128], replicated, may hold values from 96 to 384
Outputs:
- attended: bfloat16 [49152, 3072], P(('seq', 'head'))
The draws below stay inside these ranges and needn't reach their ends.
Inputs may be any that keep to these rules, and one draw needn't show every extreme that they name: `raster_to_tile`: A permutation of the slots. Raster shard d (rows d * 1536 // 8 onward, d counting seq+head) holds exactly 6 slots of every owner o, where owner o holds slots o * 1536 to (o+1) * 1536 - 1. `window_list`: row t holds t first, then 4 - 1 distinct other tiles, each within 3 tiles of t.
All inputs are finite; a program needn't handle non-finite values.
Results may differ from the reference program's by a relative error of at most 0.0036.
Values may be sent and summed in bfloat16 or wider, within the bound.
A program may use at most 64 MiB of HBM per device.

```python
import jax
import jax.numpy as jnp
from jax import lax

HEADS = 24
HEAD_DIM = 128
TILE = 384
WIN = 4
REACH = 3
TOK_DEV = 1536
TILES = 128
TOKENS = 49152
N_SEQ = 32
N_HEAD = 8


def tile_order(key):
    base = jax.random.fold_in(key, 7001)
    sources = N_SEQ * N_HEAD
    share = TOK_DEV // sources

    def owner_slots(owner):
        return owner * TOK_DEV + jax.random.permutation(jax.random.fold_in(base, owner), TOK_DEV)
    table = jax.vmap(owner_slots)(jnp.arange(N_SEQ, dtype=jnp.int32)).reshape(N_SEQ, sources, share)
    per_source = jnp.transpose(table, (1, 0, 2)).reshape(sources, N_SEQ * share)

    def shuffle(source, row):
        return jax.random.permutation(jax.random.fold_in(base, N_SEQ + source), row)
    mixed = jax.vmap(shuffle)(jnp.arange(sources, dtype=jnp.int32), per_source)
    return mixed.reshape(TOKENS).astype(jnp.int32)


def draw_raster_to_tile(key, part):
    return tile_order(key)


def draw_window_list(key, part):
    stream_key = jax.random.fold_in(key, 7003)
    tiles = jnp.arange(TILES, dtype=jnp.int32)
    offsets = jnp.concatenate([jnp.arange(-REACH, 0, dtype=jnp.int32), jnp.arange(1, REACH + 1, dtype=jnp.int32)])
    nearby = tiles[:, None] + offsets[None, :]
    scores = jax.random.randint(stream_key, (TILES, 2 * REACH), 0, 1000) * (2 * REACH) + jnp.arange(2 * REACH, dtype=jnp.int32)[None, :]
    scores = jnp.where((nearby >= 0) & (nearby < TILES), scores, -1)
    unused, picked = lax.top_k(scores, WIN - 1)
    chosen = jnp.take_along_axis(nearby, picked, axis=1)
    return jnp.concatenate([tiles[:, None], chosen], axis=1).astype(jnp.int32)


def draw_valid_count(key, part):
    stream_key = jax.random.fold_in(key, 7002)
    edges = jax.random.randint(jax.random.fold_in(stream_key, 1), (TILES,), 0, 4) == 0
    edges = edges & (jnp.arange(TILES, dtype=jnp.int32) > 0)
    shorter = jax.random.randint(jax.random.fold_in(stream_key, 2), (TILES,), TILE // 4, TILE)
    return jnp.where(edges, shorter, TILE).astype(jnp.int32)


def draw_query(key, part):
    stream_key = jax.random.fold_in(key, 7005)
    values = 2.0 * jax.random.truncated_normal(stream_key, -6.0, 6.0, (TOKENS, HEADS * HEAD_DIM))
    return values.astype(jnp.bfloat16)


def draw_key(key, part):
    stream_key = jax.random.fold_in(key, 7006)
    values = jax.random.truncated_normal(stream_key, -4.0, 4.0, (TOKENS, HEADS * HEAD_DIM))
    return values.astype(jnp.bfloat16)


def block_scale(key, extent, shards, smallest, largest):
    loudness = 1.0
    for axis_at, blocks in shards:
        steps = jax.random.uniform(jax.random.fold_in(jax.random.fold_in(key, 6), axis_at), (blocks,), jnp.float32, smallest / len(shards), largest / len(shards))
        loudness = loudness * jnp.repeat(jnp.exp(steps), extent[axis_at] // blocks).reshape((-1,) + (1,) * (len(extent) - 1 - axis_at))
    return loudness


def bell_draw(rng, shape, spread, bound, pieces=(), held_as=jnp.bfloat16):
    level = block_scale(rng, shape, pieces, -0.22, 0.18) if pieces else 1.0
    values = jax.random.normal(rng, shape, jnp.float32) * spread * level
    return jnp.minimum(jnp.maximum(values, -bound), bound).astype(held_as)


def setup_inputs(seed: int = 0) -> dict:
    arg_keys = jax.random.split(jax.random.key(seed), 7)
    return {
        "query": draw_query(jax.random.fold_in(arg_keys[6], 71), 0),
        "key": draw_key(jax.random.fold_in(arg_keys[6], 71), 0),
        "value": bell_draw(arg_keys[2], (TOKENS, HEADS * HEAD_DIM), 1.0, 6.0, ((0, 256),)),
        "raster_to_tile": draw_raster_to_tile(jax.random.fold_in(arg_keys[6], 71), 0),
        "window_list": draw_window_list(jax.random.fold_in(arg_keys[6], 71), 0),
        "valid_count": draw_valid_count(jax.random.fold_in(arg_keys[6], 71), 0),
    }


def reference(query, key, value, raster_to_tile, window_list, valid_count):
    slot_rows = jnp.zeros((TOKENS,), jnp.int32).at[raster_to_tile].set(jnp.arange(TOKENS, dtype=jnp.int32))
    q_tiles = query[slot_rows].reshape(TILES, TILE, HEADS, HEAD_DIM)
    k_tiles = key[slot_rows].reshape(TILES, TILE, HEADS, HEAD_DIM)
    v_tiles = value[slot_rows].reshape(TILES, TILE, HEADS, HEAD_DIM)
    slot_ok = jnp.arange(TILE, dtype=jnp.int32)[None, :] < valid_count[:, None]
    scale = HEAD_DIM ** -0.5

    def one_tile(index):
        wins = window_list[index]
        q_blk = q_tiles[index].astype(jnp.float32)
        k_blk = k_tiles[wins].reshape(WIN * TILE, HEADS, HEAD_DIM).astype(jnp.float32)
        v_blk = v_tiles[wins].reshape(WIN * TILE, HEADS, HEAD_DIM).astype(jnp.float32)
        usable = slot_ok[wins].reshape(WIN * TILE)
        scores = jnp.einsum("qhd,khd->hqk", q_blk, k_blk) * scale
        scores = jnp.where(usable[None, None, :], scores, -jnp.inf)
        top = jnp.max(scores, axis=2, keepdims=True)
        weights = jnp.exp(scores - top)
        total = jnp.sum(weights, axis=2)
        rounded = lax.optimization_barrier(weights.astype(jnp.bfloat16)).astype(jnp.float32)
        mixed = jnp.einsum("hqk,khd->qhd", rounded, v_blk)
        mixed = mixed / jnp.transpose(total)[:, :, None]
        mixed = jnp.where(slot_ok[index][:, None, None], mixed, 0.0)
        return mixed.astype(jnp.bfloat16).reshape(TILE, HEADS * HEAD_DIM)

    tiled = lax.map(one_tile, jnp.arange(TILES, dtype=jnp.int32)).reshape(TOKENS, HEADS * HEAD_DIM)
    return tiled[raster_to_tile]
```

```python
import functools

import jax
import jax.numpy as jnp
from jax import lax
from jax.experimental import pallas as pl
from jax.experimental.pallas import tpu as pltpu
from jax.sharding import PartitionSpec as P

MESH = pl.DeviceIdType.MESH
HEAD_DIM = 128
HEADS_HERE = 3
TILE = 384
WIN = 4
REACH = 3
TILE_DEV = 4
TOK_DEV = TILE * TILE_DEV
ROWS = 192
LAYERS = 8
OWNERS = 32
SHARE = TOK_DEV // OWNERS
EXT_TILES = TILE_DEV + 2 * REACH
LOG2E = 1.4426950408889634
FAR = -1e30
ORDER = (4, 3, 5, 2, 6, 1, 7)


def place(owner):
    chip, core = lax.div(owner, 2), lax.rem(owner, 2)
    x, step = lax.div(chip, 4), lax.rem(chip, 4)
    return x, step + lax.rem(x, 2) * (3 - 2 * step), core


def device(z, x, y, core):
    return (z * 4 + y, x * 2 + core)


def iota(shape, axis):
    return lax.broadcasted_iota(jnp.int32, shape, axis)


def bulk_wait(ref, sem):
    pltpu.make_async_copy(ref, ref, sem).wait()


def kernel(
    valid_ref, q_ref, k_ref, v_ref, meta_ref, out_ref,
    zkv, zq, zmeta, skv, sq, akv, aq, ekv0, ekv1, ekv2, tq, ot, oa, ox, orr,
    smeta, ameta, awin, win_smem, pos_col, slot_col, pos_row, slot_row,
    p1, p1t, p2, p2t,
    zkv_ss, zkv_rs, zq_ss, zq_rs, zm_ss, zm_rs,
    pkv_ss, pkv_rs, pq_ss, pq_rs, pm_ss, pm_rs,
    h_ss, hl_rs, hr_rs, po_ss, po_rs, zo_ss, zo_rs, win_s, pw_ss, pw_rs,
):
    ekv = (ekv0, ekv1, ekv2)
    seq, head = lax.axis_index("seq"), lax.axis_index("head")
    z, y = lax.div(seq, 4), lax.rem(seq, 4)
    x, core = lax.div(head, 2), lax.rem(head, 2)
    me = 2 * (4 * x + y + lax.rem(x, 2) * (3 - 2 * y)) + core

    def layer(j):
        return lax.rem(z + j, LAYERS)

    def peer(j):
        return lax.rem(me + j, OWNERS)

    def at_layer(zz):
        return device(zz, x, y, core)

    def at_owner(o):
        px, py, pc = place(o)
        return device(z, px, py, pc)

    barrier = pltpu.get_barrier_semaphore()

    @pl.loop(1, LAYERS)
    def _(j):
        pl.semaphore_signal(barrier, inc=1, device_id=at_layer(layer(j)), device_id_type=MESH)

    @pl.loop(1, OWNERS)
    def _(j):
        pl.semaphore_signal(barrier, inc=1, device_id=at_owner(peer(j)), device_id_type=MESH)

    pl.semaphore_wait(barrier, LAYERS - 1 + OWNERS - 1)

    def remote(src, dst, ss, rs, dev):
        pltpu.make_async_remote_copy(
            src_ref=src, dst_ref=dst, send_sem=ss, recv_sem=rs, device_id=dev, device_id_type=MESH
        ).start()

    my_rows = pl.ds(pl.multiple_of(z * ROWS, ROWS), ROWS)

    def z_send(src, h, dst, lanes, ss, rs):
        def columns(zz):
            return pl.ds(pl.multiple_of((zz * HEADS_HERE + h) * HEAD_DIM, HEAD_DIM), HEAD_DIM)

        for j in ORDER:
            zz = layer(j)
            remote(src.at[:, columns(zz)], dst.at[h, my_rows, lanes], ss, rs, at_layer(zz))
        pltpu.make_async_copy(src.at[:, columns(z)], dst.at[h, my_rows, lanes], rs).start()

    def z_send_kv(h):
        z_send(k_ref, h, zkv, pl.ds(0, HEAD_DIM), zkv_ss.at[h], zkv_rs.at[h])
        z_send(v_ref, h, zkv, pl.ds(HEAD_DIM, HEAD_DIM), zkv_ss.at[h], zkv_rs.at[h])

    def z_send_q(h):
        z_send(q_ref, h, zq, pl.ds(0, HEAD_DIM), zq_ss.at[h], zq_rs.at[h])

    my_share = pl.ds(pl.multiple_of(me * SHARE, SHARE), SHARE)

    def share(o):
        return pl.ds(pl.multiple_of(o * SHARE, SHARE), SHARE)

    def plane_send(src, dst, ss, rs):
        @pl.loop(1, OWNERS)
        def _(j):
            o = peer(j)
            remote(src.at[share(o)], dst.at[my_share], ss, rs, at_owner(o))

        pltpu.make_async_copy(src.at[my_share], dst.at[my_share], rs).start()

    def permute(table, src, dst, block=512):
        @pl.loop(0, TOK_DEV // block)
        def _(i):
            rows = pl.ds(pl.multiple_of(i * block, block), block)
            dst[rows, :] = jnp.dot(
                table[rows, :], src[...], preferred_element_type=jnp.float32
            ).astype(jnp.bfloat16)

    for j in ORDER:
        zz = layer(j)
        remote(meta_ref, zmeta.at[z], zm_ss, zm_rs, at_layer(zz))
    pltpu.make_async_copy(meta_ref, zmeta.at[z], zm_rs).start()
    z_send_kv(0)
    z_send_kv(1)

    bulk_wait(zmeta, zm_rs)

    @pl.loop(0, LAYERS)
    def _(s):
        row = zmeta[s][:, 0:256].astype(jnp.float32)
        wide = jnp.broadcast_to(row, (ROWS, 256))
        diag = iota((ROWS, 256), 0) == iota((ROWS, 256), 1)
        col = jnp.sum(jnp.where(diag, wide, 0.0), axis=1, keepdims=True)
        rank = jnp.sum(jnp.where(wide < col, 1.0, 0.0), axis=1, keepdims=True)
        owner = jnp.floor((col + 0.5) * (1.0 / TOK_DEV))
        pos = owner * (SHARE - 6.0) + rank + (6 * s).astype(jnp.float32)
        rows = pl.ds(pl.multiple_of(s * ROWS, ROWS), ROWS)
        pos_col[rows, :] = jnp.broadcast_to(pos, (ROWS, 128))
        slot_col[rows, :] = jnp.broadcast_to(col, (ROWS, 128))

    def to_row(col_ref, row_ref):
        for b in range(TOK_DEV // 128):
            block = col_ref[b * 128 : (b + 1) * 128, :]
            diag = iota((128, 128), 0) == iota((128, 128), 1)
            row_ref[:, b * 128 : (b + 1) * 128] = jnp.sum(
                jnp.where(diag, block, 0.0), axis=0, keepdims=True
            )

    to_row(pos_col, pos_row)
    to_row(slot_col, slot_row)

    def table_by_row(table, row_ref, sorted_ref):
        @pl.loop(0, TOK_DEV // 64)
        def _(b):
            rows = pl.ds(pl.multiple_of(b * 64, 64), 64)
            want = (iota((64, TOK_DEV), 0) + b * 64).astype(jnp.float32)
            hit = want == row_ref[...]
            table[rows, :] = jnp.where(hit, 1.0, 0.0).astype(jnp.bfloat16)
            if sorted_ref is not None:
                slot = jnp.sum(jnp.where(hit, slot_row[...], 0.0), axis=1, keepdims=True)
                sorted_ref[rows, :] = jnp.broadcast_to(slot, (64, 128))

    def table_by_col(table, col_ref):
        @pl.loop(0, TOK_DEV // 64)
        def _(b):
            rows = pl.ds(pl.multiple_of(b * 64, 64), 64)
            want = iota((64, TOK_DEV), 1).astype(jnp.float32)
            hit = want == col_ref[rows, 0:1]
            table[rows, :] = jnp.where(hit, 1.0, 0.0).astype(jnp.bfloat16)

    table_by_row(p1, pos_row, slot_col)

    def window_of(o):
        return zmeta.at[lax.div(o, 4), :, pl.ds(256, 128)]

    @pl.loop(0, OWNERS)
    def _(o):
        block = slot_col[share(o), :]
        diag = iota((SHARE, 128), 0) == iota((SHARE, 128), 1)
        smeta[o] = jnp.sum(jnp.where(diag, block, 0.0), axis=0, keepdims=True)

    @pl.loop(1, OWNERS)
    def _(j):
        o = peer(j)
        remote(smeta.at[o], ameta.at[me], pm_ss, pm_rs, at_owner(o))
        remote(window_of(o), awin.at[me], pw_ss, pw_rs, at_owner(o))

    pltpu.make_async_copy(smeta.at[me], ameta.at[me], pm_rs).start()
    pltpu.make_async_copy(window_of(me), awin.at[me], pw_rs).start()

    table_by_col(p1t, pos_col)

    bulk_wait(ameta, pm_rs)
    bulk_wait(awin, pw_rs)
    window_row = pltpu.make_async_copy(awin.at[2 * lax.rem(me, 4)], win_smem, win_s)
    window_row.start()

    @pl.loop(0, OWNERS)
    def _(o):
        row = ameta[o]
        wide = jnp.broadcast_to(row, (SHARE, 128))
        diag = iota((SHARE, 128), 0) == iota((SHARE, 128), 1)
        col = jnp.sum(jnp.where(diag, wide, 0.0), axis=1, keepdims=True)
        col = col - (me * TOK_DEV).astype(jnp.float32)
        pos_col[share(o), :] = jnp.broadcast_to(col, (SHARE, 128))

    to_row(pos_col, pos_row)
    table_by_row(p2, pos_row, None)
    table_by_col(p2t, pos_col)
    window_row.wait()

    def sort_kv(h):
        bulk_wait(zkv.at[h], zkv_rs.at[h])
        permute(p1, zkv.at[h], skv.at[h])
        plane_send(skv.at[h], akv.at[h], pkv_ss.at[h], pkv_rs.at[h])

    def sort_q(h):
        bulk_wait(zq.at[h], zq_rs.at[h])
        permute(p1, zq.at[h], sq.at[h])
        plane_send(sq.at[h], aq.at[h], pq_ss.at[h], pq_rs.at[h])

    not_first, not_last = me > 0, me < OWNERS - 1

    def halo_copies(h):
        to_right = pltpu.make_async_remote_copy(
            src_ref=ekv[h].at[pl.ds(REACH + 1, REACH)],
            dst_ref=ekv[h].at[pl.ds(0, REACH)],
            send_sem=h_ss.at[0, h],
            recv_sem=hl_rs.at[h],
            device_id=at_owner(lax.rem(me + 1, OWNERS)),
            device_id_type=MESH,
        )
        to_left = pltpu.make_async_remote_copy(
            src_ref=ekv[h].at[pl.ds(REACH, REACH)],
            dst_ref=ekv[h].at[pl.ds(REACH + TILE_DEV, REACH)],
            send_sem=h_ss.at[1, h],
            recv_sem=hr_rs.at[h],
            device_id=at_owner(lax.rem(me + OWNERS - 1, OWNERS)),
            device_id_type=MESH,
        )
        return to_right, to_left

    def tile_kv(h):
        bulk_wait(akv.at[h], pkv_rs.at[h])

        @pl.loop(0, TILE_DEV)
        def _(t):
            rows = pl.ds(pl.multiple_of(t * TILE, TILE), TILE)
            ekv[h][REACH + t] = jnp.dot(
                p2[rows, :], akv[h], preferred_element_type=jnp.float32
            ).astype(jnp.bfloat16)

        to_right, to_left = halo_copies(h)

        @pl.when(not_last)
        def _():
            to_right.start()

        @pl.when(not_first)
        def _():
            to_left.start()

    def halo_wait(h):
        to_right, to_left = halo_copies(h)

        @pl.when(not_first)
        def _():
            to_right.wait_recv()

        @pl.when(not_last)
        def _():
            to_left.wait_recv()

    factor = HEAD_DIM**-0.5 * LOG2E
    QB = 192

    def attend(h):
        bulk_wait(aq.at[h], pq_rs.at[h])
        permute(p2, aq.at[h], tq)
        halo_wait(h)

        @pl.loop(0, TILE_DEV)
        def _(t):
            starts, biases = [], []
            for w in range(WIN):
                tile = win_smem[0, SHARE + t * WIN + w]
                starts.append(lax.clamp(0, tile - (me * TILE_DEV - REACH), EXT_TILES - 1))
                biases.append(jnp.where(iota((1, TILE), 1) < valid_ref[tile], 0.0, FAR))
            real = valid_ref[me * TILE_DEV + t]
            for b in range(TILE // QB):
                rows = pl.ds(pl.multiple_of(t * TILE + b * QB, QB), QB)
                query = tq[rows, :]
                scores = []
                for w in range(WIN):
                    keys = ekv[h][starts[w], :, 0:HEAD_DIM]
                    scores.append(
                        lax.dot_general(
                            query, keys, (((1,), (1,)), ((), ())), preferred_element_type=jnp.float32
                        )
                        + biases[w]
                    )
                top = functools.reduce(
                    jnp.maximum, [jnp.max(s, axis=1, keepdims=True) for s in scores]
                )
                weights = [jnp.exp2((s - top) * factor) for s in scores]
                total = functools.reduce(
                    jnp.add, [jnp.sum(p, axis=1, keepdims=True) for p in weights]
                )
                mixed = None
                for w in range(WIN):
                    values = ekv[h][starts[w], :, HEAD_DIM : 2 * HEAD_DIM]
                    term = jnp.dot(
                        weights[w].astype(jnp.bfloat16), values, preferred_element_type=jnp.float32
                    )
                    mixed = term if mixed is None else mixed + term
                mixed = mixed / total
                keep = iota((QB, 1), 0) + b * QB < real
                ot[rows, :] = jnp.where(keep, mixed, 0.0).astype(jnp.bfloat16)

        permute(p2t, ot, oa.at[h])
        plane_send(oa.at[h], ox.at[h], po_ss.at[h], po_rs.at[h])

    def give_back(h):
        bulk_wait(ox.at[h], po_rs.at[h])
        permute(p1t, ox.at[h], orr.at[h])
        columns = pl.ds(pl.multiple_of((z * HEADS_HERE + h) * HEAD_DIM, HEAD_DIM), HEAD_DIM)
        for j in ORDER:
            zz = layer(j)
            rows = pl.ds(pl.multiple_of(zz * ROWS, ROWS), ROWS)
            remote(orr.at[h, rows], out_ref.at[:, columns], zo_ss.at[h], zo_rs.at[h], at_layer(zz))
        pltpu.make_async_copy(orr.at[h, my_rows], out_ref.at[:, columns], zo_rs.at[h]).start()

    sort_kv(0)
    z_send_kv(2)
    tile_kv(0)
    sort_kv(1)
    z_send_q(0)
    z_send_q(1)
    tile_kv(1)
    sort_kv(2)
    z_send_q(2)
    sort_q(0)
    tile_kv(2)
    sort_q(1)
    attend(0)
    sort_q(2)
    give_back(0)
    attend(1)
    give_back(1)
    attend(2)
    give_back(2)

    bulk_wait(zmeta.at[pl.ds(0, LAYERS - 1)], zm_ss)
    bulk_wait(smeta.at[pl.ds(0, OWNERS - 1)], pm_ss)
    bulk_wait(awin.at[pl.ds(0, OWNERS - 1)], pw_ss)
    z_sent = pl.ds(0, (LAYERS - 1) * ROWS)
    plane_sent = pl.ds(0, (OWNERS - 1) * SHARE)
    for h in range(HEADS_HERE):
        bulk_wait(zkv.at[h, z_sent], zkv_ss.at[h])
        bulk_wait(zq.at[h, z_sent], zq_ss.at[h])
        bulk_wait(skv.at[h, plane_sent], pkv_ss.at[h])
        bulk_wait(sq.at[h, plane_sent], pq_ss.at[h])
        bulk_wait(oa.at[h, plane_sent], po_ss.at[h])
        bulk_wait(orr.at[h, z_sent], zo_ss.at[h])
        to_right, to_left = halo_copies(h)

        @pl.when(not_last)
        def _():
            to_right.wait_send()

        @pl.when(not_first)
        def _():
            to_left.wait_send()

        bulk_wait(out_ref.at[:, pl.ds(0, LAYERS * HEAD_DIM)], zo_rs.at[h])


def body(query, key, value, raster_to_tile, window_list, valid_count):
    meta = jnp.concatenate(
        [
            raster_to_tile,
            jnp.full((256 - ROWS,), 1 << 20, jnp.int32),
            jnp.zeros((SHARE,), jnp.int32),
            window_list.reshape(-1),
            jnp.zeros((128 - SHARE - TILE_DEV * WIN,), jnp.int32),
        ]
    ).reshape(1, 384)
    heads, bf16, dma = HEADS_HERE, jnp.bfloat16, pltpu.SemaphoreType.DMA
    vmem = pltpu.VMEM
    kv, one = 2 * HEAD_DIM, HEAD_DIM
    scratch = [
        vmem((heads, TOK_DEV, kv), bf16),
        vmem((heads, TOK_DEV, one), bf16),
        vmem((LAYERS, 1, 384), jnp.int32),
        vmem((heads, TOK_DEV, kv), bf16),
        vmem((heads, TOK_DEV, one), bf16),
        vmem((heads, TOK_DEV, kv), bf16),
        vmem((heads, TOK_DEV, one), bf16),
        vmem((EXT_TILES, TILE, kv), bf16),
        vmem((EXT_TILES, TILE, kv), bf16),
        vmem((EXT_TILES, TILE, kv), bf16),
        vmem((TOK_DEV, one), bf16),
        vmem((TOK_DEV, one), bf16),
        vmem((heads, TOK_DEV, one), bf16),
        vmem((heads, TOK_DEV, one), bf16),
        vmem((heads, TOK_DEV, one), bf16),
        vmem((OWNERS, 1, 128), jnp.float32),
        vmem((OWNERS, 1, 128), jnp.float32),
        vmem((OWNERS, 1, 128), jnp.int32),
        pltpu.SMEM((1, 128), jnp.int32),
        vmem((TOK_DEV, 128), jnp.float32),
        vmem((TOK_DEV, 128), jnp.float32),
        vmem((1, TOK_DEV), jnp.float32),
        vmem((1, TOK_DEV), jnp.float32),
        vmem((TOK_DEV, TOK_DEV), bf16),
        vmem((TOK_DEV, TOK_DEV), bf16),
        vmem((TOK_DEV, TOK_DEV), bf16),
        vmem((TOK_DEV, TOK_DEV), bf16),
        dma((heads,)), dma((heads,)), dma((heads,)), dma((heads,)), dma, dma,
        dma((heads,)), dma((heads,)), dma((heads,)), dma((heads,)), dma, dma,
        dma((2, heads)), dma((heads,)), dma((heads,)),
        dma((heads,)), dma((heads,)), dma((heads,)), dma((heads,)), dma, dma, dma,
    ]
    anywhere = pl.BlockSpec(memory_space=pl.ANY)
    return pl.pallas_call(
        kernel,
        out_shape=jax.ShapeDtypeStruct(query.shape, query.dtype),
        in_specs=[
            pl.BlockSpec(memory_space=pltpu.SMEM),
            anywhere,
            anywhere,
            anywhere,
            pl.BlockSpec(memory_space=vmem),
        ],
        out_specs=anywhere,
        scratch_shapes=scratch,
        compiler_params=pltpu.CompilerParams(
            collective_id=0, has_side_effects=True, vmem_limit_bytes=58 * 2**20
        ),
    )(valid_count, query, key, value, meta)


def solution(mesh):
    placed = (
        P(("seq", "head"), None),
        P(("seq", "head"), None),
        P(("seq", "head"), None),
        P(("seq", "head")),
        P("seq", None),
        P(),
    )
    return jax.shard_map(
        body, mesh=mesh, in_specs=placed, out_specs=P(("seq", "head"), None), check_vma=False
    )
```

```python
import functools

import jax
import jax.numpy as jnp
from jax import lax
from jax.experimental import pallas as pl
from jax.experimental.pallas import tpu as pltpu
from jax.sharding import PartitionSpec as P

MESH = pl.DeviceIdType.MESH
HEAD_DIM = 128
HEADS_HERE = 3
TILE = 384
WIN = 4
REACH = 3
TILE_DEV = 4
TOK_DEV = TILE * TILE_DEV
ROWS = 192
LAYERS = 8
OWNERS = 32
SHARE = TOK_DEV // OWNERS
EXT_TILES = TILE_DEV + 2 * REACH
LOG2E = 1.4426950408889634
FAR = -1e30
ORDER = (4, 3, 5, 2, 6, 1, 7)


def place(owner):
    chip, core = lax.div(owner, 2), lax.rem(owner, 2)
    x, step = lax.div(chip, 4), lax.rem(chip, 4)
    return x, step + lax.rem(x, 2) * (3 - 2 * step), core


def device(z, x, y, core):
    return (z * 4 + y, x * 2 + core)


def iota(shape, axis):
    return lax.broadcasted_iota(jnp.int32, shape, axis)


def bulk_wait(ref, sem):
    pltpu.make_async_copy(ref, ref, sem).wait()


def kernel(
    valid_ref, q_ref, k_ref, v_ref, slots_ref, windows_ref, out_ref,
    zkv, zq, zmeta, zwin, skv, sq, akv, aq, ekv, ekw, tq, ot, oa, ox, orr,
    smeta, ameta, awin, win_smem, pos_col, slot_col, pos_row, slot_row, tile_col, tile_row,
    p1, p1t, p2, p2t,
    zkv_ss, zkv_rs, zq_ss, zq_rs, zm_ss, zm_rs,
    pkv_ss, pkv_rs, pq_ss, pq_rs, pm_ss, pm_rs,
    h_ss, hl_rs, hr_rs, po_ss, po_rs, zo_ss, zo_rs, win_s, pw_ss, pw_rs, zw_ss, zw_rs,
):
    seq, head = lax.axis_index("seq"), lax.axis_index("head")
    z, y = lax.div(seq, 4), lax.rem(seq, 4)
    x, core = lax.div(head, 2), lax.rem(head, 2)
    me = 2 * (4 * x + y + lax.rem(x, 2) * (3 - 2 * y)) + core

    def layer(j):
        return lax.rem(z + j, LAYERS)

    def peer(j):
        return lax.rem(me + j, OWNERS)

    def at_layer(zz):
        return device(zz, x, y, core)

    def at_owner(o):
        px, py, pc = place(o)
        return device(z, px, py, pc)

    barrier = pltpu.get_barrier_semaphore()

    @pl.loop(1, LAYERS)
    def _(j):
        pl.semaphore_signal(barrier, inc=1, device_id=at_layer(layer(j)), device_id_type=MESH)

    @pl.loop(1, OWNERS)
    def _(j):
        pl.semaphore_signal(barrier, inc=1, device_id=at_owner(peer(j)), device_id_type=MESH)

    pl.semaphore_wait(barrier, LAYERS - 1 + OWNERS - 1)

    def remote(src, dst, ss, rs, dev):
        pltpu.make_async_remote_copy(
            src_ref=src, dst_ref=dst, send_sem=ss, recv_sem=rs, device_id=dev, device_id_type=MESH
        ).start()

    my_rows = pl.ds(pl.multiple_of(z * ROWS, ROWS), ROWS)

    def z_send(src, h, dst, lanes, ss, rs):
        def columns(zz):
            return pl.ds(pl.multiple_of((zz * HEADS_HERE + h) * HEAD_DIM, HEAD_DIM), HEAD_DIM)

        for j in ORDER:
            zz = layer(j)
            remote(src.at[:, columns(zz)], dst.at[h, my_rows, lanes], ss, rs, at_layer(zz))
        pltpu.make_async_copy(src.at[:, columns(z)], dst.at[h, my_rows, lanes], rs).start()

    def z_send_kv(h):
        z_send(k_ref, h, zkv, pl.ds(0, HEAD_DIM), zkv_ss.at[h], zkv_rs.at[h])
        z_send(v_ref, h, zkv, pl.ds(HEAD_DIM, HEAD_DIM), zkv_ss.at[h], zkv_rs.at[h])

    def z_send_q(h):
        z_send(q_ref, h, zq, pl.ds(0, HEAD_DIM), zq_ss.at[h], zq_rs.at[h])

    my_share = pl.ds(pl.multiple_of(me * SHARE, SHARE), SHARE)

    def share(o):
        return pl.ds(pl.multiple_of(o * SHARE, SHARE), SHARE)

    def plane_send(src, dst, ss, rs):
        @pl.loop(1, OWNERS)
        def _(j):
            o = peer(j)
            remote(src.at[share(o)], dst.at[my_share], ss, rs, at_owner(o))

        pltpu.make_async_copy(src.at[my_share], dst.at[my_share], rs).start()

    def permute(table, src, store, block=512, depth=256):
        @pl.loop(0, TOK_DEV // block)
        def _(i):
            rows = pl.ds(pl.multiple_of(i * block, block), block)
            total = None
            for k in range(0, TOK_DEV, depth):
                term = jnp.dot(
                    table[rows, k : k + depth],
                    src[k : k + depth, :],
                    preferred_element_type=jnp.float32,
                )
                total = term if total is None else total + term
            store(i, rows, total.astype(jnp.bfloat16))

    def into(ref):
        def store(i, rows, value):
            ref[rows, :] = value

        return store

    for j in ORDER:
        zz = layer(j)
        remote(slots_ref, zmeta.at[z], zm_ss, zm_rs, at_layer(zz))
        remote(windows_ref, zwin.at[z], zw_ss, zw_rs, at_layer(zz))
    pltpu.make_async_copy(slots_ref, zmeta.at[z], zm_rs).start()
    pltpu.make_async_copy(windows_ref, zwin.at[z], zw_rs).start()
    z_send_kv(0)
    z_send_q(0)
    z_send_kv(1)
    z_send_q(1)
    z_send_kv(2)
    z_send_q(2)

    bulk_wait(zmeta, zm_rs)

    @pl.loop(0, LAYERS)
    def _(s):
        wide = jnp.broadcast_to(zmeta[s].astype(jnp.float32), (ROWS, ROWS))
        diag = iota((ROWS, ROWS), 0) == iota((ROWS, ROWS), 1)
        col = jnp.sum(jnp.where(diag, wide, 0.0), axis=1, keepdims=True)
        rank = jnp.sum(jnp.where(wide < col, 1.0, 0.0), axis=1, keepdims=True)
        owner = jnp.floor((col + 0.5) * (1.0 / TOK_DEV))
        pos = owner * (SHARE - 6.0) + rank + (6 * s).astype(jnp.float32)
        rows = pl.ds(pl.multiple_of(s * ROWS, ROWS), ROWS)
        pos_col[rows, :] = jnp.broadcast_to(pos, (ROWS, 128))
        slot_col[rows, :] = jnp.broadcast_to(col, (ROWS, 128))

    def to_row(col_ref, row_ref):
        for b in range(TOK_DEV // 128):
            block = col_ref[b * 128 : (b + 1) * 128, :]
            diag = iota((128, 128), 0) == iota((128, 128), 1)
            row_ref[:, b * 128 : (b + 1) * 128] = jnp.sum(
                jnp.where(diag, block, 0.0), axis=0, keepdims=True
            )

    to_row(pos_col, pos_row)
    to_row(slot_col, slot_row)

    def table_by_row(table, row_ref, sorted_ref):
        @pl.loop(0, TOK_DEV // 64)
        def _(b):
            rows = pl.ds(pl.multiple_of(b * 64, 64), 64)
            want = (iota((64, TOK_DEV), 0) + b * 64).astype(jnp.float32)
            hit = want == row_ref[...]
            table[rows, :] = jnp.where(hit, 1.0, 0.0).astype(jnp.bfloat16)
            if sorted_ref is not None:
                slot = jnp.sum(jnp.where(hit, slot_row[...], 0.0), axis=1, keepdims=True)
                sorted_ref[rows, :] = jnp.broadcast_to(slot, (64, 128))

    def table_by_col(table, col_ref):
        @pl.loop(0, TOK_DEV // 64)
        def _(b):
            rows = pl.ds(pl.multiple_of(b * 64, 64), 64)
            want = iota((64, TOK_DEV), 1).astype(jnp.float32)
            hit = want == col_ref[rows, 0:1]
            table[rows, :] = jnp.where(hit, 1.0, 0.0).astype(jnp.bfloat16)

    def window_of(o):
        return zwin.at[lax.div(o, 4)]

    window_row = pltpu.make_async_copy(awin.at[2 * lax.rem(me, 4)], win_smem, win_s)

    def send_slots():
        table_by_row(p1, pos_row, slot_col)
        bulk_wait(zwin, zw_rs)

        @pl.loop(0, OWNERS)
        def _(o):
            block = slot_col[share(o), :]
            diag = iota((SHARE, 128), 0) == iota((SHARE, 128), 1)
            smeta[o] = jnp.sum(jnp.where(diag, block, 0.0), axis=0, keepdims=True)

        @pl.loop(1, OWNERS)
        def _(j):
            o = peer(j)
            remote(smeta.at[o], ameta.at[me], pm_ss, pm_rs, at_owner(o))
            remote(window_of(o), awin.at[me], pw_ss, pw_rs, at_owner(o))

        pltpu.make_async_copy(smeta.at[me], ameta.at[me], pm_rs).start()
        pltpu.make_async_copy(window_of(me), awin.at[me], pw_rs).start()

    def take_slots():
        bulk_wait(ameta, pm_rs)
        bulk_wait(awin, pw_rs)
        window_row.start()

        @pl.loop(0, OWNERS)
        def _(o):
            wide = jnp.broadcast_to(ameta[o], (SHARE, 128))
            diag = iota((SHARE, 128), 0) == iota((SHARE, 128), 1)
            col = jnp.sum(jnp.where(diag, wide, 0.0), axis=1, keepdims=True)
            col = col - (me * TOK_DEV).astype(jnp.float32)
            tile_col[share(o), :] = jnp.broadcast_to(col, (SHARE, 128))

        to_row(tile_col, tile_row)
        table_by_row(p2, tile_row, None)
        window_row.wait()

    def back_from_tiles():
        table_by_col(p2t, tile_col)

    def back_from_owners():
        table_by_col(p1t, pos_col)

    def sort_kv(h):
        bulk_wait(zkv.at[h], zkv_rs.at[h])
        permute(p1, zkv.at[h], into(skv.at[h]))
        plane_send(skv.at[h], akv.at[h], pkv_ss.at[h], pkv_rs.at[h])

    def sort_q(h):
        bulk_wait(zq.at[h], zq_rs.at[h])
        permute(p1, zq.at[h], into(sq.at[h]))
        plane_send(sq.at[h], aq.at[h], pq_ss.at[h], pq_rs.at[h])

    not_first, not_last = me > 0, me < OWNERS - 1

    def halo_copies(h):
        to_right = pltpu.make_async_remote_copy(
            src_ref=ekv.at[h, pl.ds(REACH + 1, REACH)],
            dst_ref=ekv.at[h, pl.ds(0, REACH)],
            send_sem=h_ss.at[0, h],
            recv_sem=hl_rs.at[h],
            device_id=at_owner(lax.rem(me + 1, OWNERS)),
            device_id_type=MESH,
        )
        to_left = pltpu.make_async_remote_copy(
            src_ref=ekv.at[h, pl.ds(REACH, REACH)],
            dst_ref=ekv.at[h, pl.ds(REACH + TILE_DEV, REACH)],
            send_sem=h_ss.at[1, h],
            recv_sem=hr_rs.at[h],
            device_id=at_owner(lax.rem(me + OWNERS - 1, OWNERS)),
            device_id_type=MESH,
        )
        return to_right, to_left

    def tile_kv(h):
        bulk_wait(akv.at[h], pkv_rs.at[h])

        def store(t, rows, value):
            ekv[h, REACH + t] = value

        permute(p2, akv.at[h], store, block=TILE)
        to_right, to_left = halo_copies(h)

        @pl.when(not_last)
        def _():
            to_right.start()

        @pl.when(not_first)
        def _():
            to_left.start()

    def halo_wait(h):
        to_right, to_left = halo_copies(h)

        @pl.when(not_first)
        def _():
            to_right.wait_recv()

        @pl.when(not_last)
        def _():
            to_left.wait_recv()

    factor = HEAD_DIM**-0.5 * LOG2E

    def tile_q(h):
        bulk_wait(aq.at[h], pq_rs.at[h])
        permute(p2, aq.at[h], into(tq.at[h]))

    def attend(h):
        halo_wait(h)

        @pl.loop(0, EXT_TILES)
        def _(e):
            ekw[e] = ekv[h, e]

        @pl.loop(0, TILE_DEV)
        def _(t):
            starts, biases = [], []
            for w in range(WIN):
                tile = win_smem[t, w]
                starts.append(lax.clamp(0, tile - (me * TILE_DEV - REACH), EXT_TILES - 1))
                biases.append(jnp.where(iota((1, TILE), 1) < valid_ref[tile], 0.0, FAR))
            real = valid_ref[me * TILE_DEV + t]
            rows = pl.ds(pl.multiple_of(t * TILE, TILE), TILE)
            query = tq[h, rows, :]
            scores = []
            for w in range(WIN):
                keys = ekw[starts[w], :, 0:HEAD_DIM]
                scores.append(
                    lax.dot_general(
                        query, keys, (((1,), (1,)), ((), ())), preferred_element_type=jnp.float32
                    )
                    + biases[w]
                )
            top = functools.reduce(
                jnp.maximum, [jnp.max(s, axis=1, keepdims=True) for s in scores]
            )
            weights = [jnp.exp2((s - top) * factor) for s in scores]
            total = functools.reduce(
                jnp.add, [jnp.sum(p, axis=1, keepdims=True) for p in weights]
            )
            mixed = None
            for w in range(WIN):
                values = ekw[starts[w], :, HEAD_DIM : 2 * HEAD_DIM]
                term = jnp.dot(
                    weights[w].astype(jnp.bfloat16), values, preferred_element_type=jnp.float32
                )
                mixed = term if mixed is None else mixed + term
            mixed = mixed / total
            keep = iota((TILE, 1), 0) < real
            ot[rows, :] = jnp.where(keep, mixed, 0.0).astype(jnp.bfloat16)

    def send_back(h):
        permute(p2t, ot, into(oa.at[h]))
        plane_send(oa.at[h], ox.at[h], po_ss.at[h], po_rs.at[h])

    def unsort(h):
        bulk_wait(ox.at[h], po_rs.at[h])
        permute(p1t, ox.at[h], into(orr.at[h]))

    def give_back(h):
        columns = pl.ds(pl.multiple_of((z * HEADS_HERE + h) * HEAD_DIM, HEAD_DIM), HEAD_DIM)
        for j in ORDER:
            zz = layer(j)
            rows = pl.ds(pl.multiple_of(zz * ROWS, ROWS), ROWS)
            remote(orr.at[h, rows], out_ref.at[:, columns], zo_ss.at[h], zo_rs.at[h], at_layer(zz))
        pltpu.make_async_copy(orr.at[h, my_rows], out_ref.at[:, columns], zo_rs.at[h]).start()

    send_slots()
    take_slots()
    sort_kv(0)
    back_from_tiles()
    back_from_owners()
    sort_q(0)
    tile_kv(0)
    tile_q(0)
    sort_kv(1)
    attend(0)
    send_back(0)
    sort_q(1)
    tile_kv(1)
    tile_q(1)
    unsort(0)
    sort_kv(2)
    attend(1)
    sort_q(2)
    give_back(0)
    tile_kv(2)
    tile_q(2)
    send_back(1)
    attend(2)
    send_back(2)
    unsort(1)
    give_back(1)
    unsort(2)
    give_back(2)

    bulk_wait(zmeta.at[pl.ds(0, LAYERS - 1)], zm_ss)
    bulk_wait(zwin.at[pl.ds(0, LAYERS - 1)], zw_ss)
    bulk_wait(smeta.at[pl.ds(0, OWNERS - 1)], pm_ss)
    bulk_wait(awin.at[pl.ds(0, OWNERS - 1)], pw_ss)
    z_sent = pl.ds(0, (LAYERS - 1) * ROWS)
    plane_sent = pl.ds(0, (OWNERS - 1) * SHARE)
    for h in range(HEADS_HERE):
        bulk_wait(zkv.at[h, z_sent], zkv_ss.at[h])
        bulk_wait(zq.at[h, z_sent], zq_ss.at[h])
        bulk_wait(skv.at[h, plane_sent], pkv_ss.at[h])
        bulk_wait(sq.at[h, plane_sent], pq_ss.at[h])
        bulk_wait(oa.at[h, plane_sent], po_ss.at[h])
        bulk_wait(orr.at[h, z_sent], zo_ss.at[h])
        to_right, to_left = halo_copies(h)

        @pl.when(not_last)
        def _():
            to_right.wait_send()

        @pl.when(not_first)
        def _():
            to_left.wait_send()

        bulk_wait(out_ref.at[:, pl.ds(0, LAYERS * HEAD_DIM)], zo_rs.at[h])


def body(query, key, value, raster_to_tile, window_list, valid_count):
    heads, bf16, dma = HEADS_HERE, jnp.bfloat16, pltpu.SemaphoreType.DMA
    vmem = pltpu.VMEM
    kv, one = 2 * HEAD_DIM, HEAD_DIM
    scratch = [
        vmem((heads, TOK_DEV, kv), bf16),
        vmem((heads, TOK_DEV, one), bf16),
        vmem((LAYERS, 1, ROWS), jnp.int32),
        vmem((LAYERS, TILE_DEV, WIN), jnp.int32),
        vmem((heads, TOK_DEV, kv), bf16),
        vmem((heads, TOK_DEV, one), bf16),
        vmem((heads, TOK_DEV, kv), bf16),
        vmem((heads, TOK_DEV, one), bf16),
        vmem((heads, EXT_TILES, TILE, kv), bf16),
        vmem((EXT_TILES, TILE, kv), bf16),
        vmem((heads, TOK_DEV, one), bf16),
        vmem((TOK_DEV, one), bf16),
        vmem((heads, TOK_DEV, one), bf16),
        vmem((heads, TOK_DEV, one), bf16),
        vmem((heads, TOK_DEV, one), bf16),
        vmem((OWNERS, 1, 128), jnp.float32),
        vmem((OWNERS, 1, 128), jnp.float32),
        vmem((OWNERS, TILE_DEV, WIN), jnp.int32),
        pltpu.SMEM((TILE_DEV, WIN), jnp.int32),
        vmem((TOK_DEV, 128), jnp.float32),
        vmem((TOK_DEV, 128), jnp.float32),
        vmem((1, TOK_DEV), jnp.float32),
        vmem((1, TOK_DEV), jnp.float32),
        vmem((TOK_DEV, 128), jnp.float32),
        vmem((1, TOK_DEV), jnp.float32),
        vmem((TOK_DEV, TOK_DEV), bf16),
        vmem((TOK_DEV, TOK_DEV), bf16),
        vmem((TOK_DEV, TOK_DEV), bf16),
        vmem((TOK_DEV, TOK_DEV), bf16),
        dma((heads,)), dma((heads,)), dma((heads,)), dma((heads,)), dma, dma,
        dma((heads,)), dma((heads,)), dma((heads,)), dma((heads,)), dma, dma,
        dma((2, heads)), dma((heads,)), dma((heads,)),
        dma((heads,)), dma((heads,)), dma((heads,)), dma((heads,)), dma, dma, dma, dma, dma,
    ]
    anywhere = pl.BlockSpec(memory_space=pl.ANY)
    return pl.pallas_call(
        kernel,
        out_shape=jax.ShapeDtypeStruct(query.shape, query.dtype),
        in_specs=[
            pl.BlockSpec(memory_space=pltpu.SMEM),
            anywhere,
            anywhere,
            anywhere,
            pl.BlockSpec(memory_space=vmem),
            pl.BlockSpec(memory_space=vmem),
        ],
        out_specs=anywhere,
        scratch_shapes=scratch,
        compiler_params=pltpu.CompilerParams(
            collective_id=0, has_side_effects=True, vmem_limit_bytes=58 * 2**20
        ),
    )(valid_count, query, key, value, raster_to_tile.reshape(1, ROWS), window_list)


def solution(mesh):
    placed = (
        P(("seq", "head"), None),
        P(("seq", "head"), None),
        P(("seq", "head"), None),
        P(("seq", "head")),
        P("seq", None),
        P(),
    )
    return jax.shard_map(
        body, mesh=mesh, in_specs=placed, out_specs=P(("seq", "head"), None), check_vma=False
    )
```

```python
import functools

import jax
import jax.numpy as jnp
from jax import lax
from jax.experimental import pallas as pl
from jax.experimental.pallas import tpu as pltpu
from jax.sharding import PartitionSpec as P

MESH = pl.DeviceIdType.MESH
HEAD_DIM = 128
HEADS_HERE = 3
TILE = 384
WIN = 4
REACH = 3
TILE_DEV = 4
TOK_DEV = TILE * TILE_DEV
ROWS = 192
LAYERS = 8
OWNERS = 32
SHARE = TOK_DEV // OWNERS
EXT_TILES = TILE_DEV + 2 * REACH
LOG2E = 1.4426950408889634
FAR = -1e30
ORDER = (4, 3, 5, 2, 6, 1, 7)


def place(owner):
    chip, core = lax.div(owner, 2), lax.rem(owner, 2)
    x, step = lax.div(chip, 4), lax.rem(chip, 4)
    return x, step + lax.rem(x, 2) * (3 - 2 * step), core


def device(z, x, y, core):
    return (z * 4 + y, x * 2 + core)


def iota(shape, axis):
    return lax.broadcasted_iota(jnp.int32, shape, axis)


def bulk_wait(ref, sem):
    pltpu.make_async_copy(ref, ref, sem).wait()


def kernel(
    valid_ref, q_ref, k_ref, v_ref, slots_ref, windows_ref, out_ref,
    zkv, zq, zmeta, zwin, skv, sq, akv, aq, ekv, ekw, tq, ot, oa, ox, orr,
    smeta, ameta, awin, win_smem, pos_col, slot_col, pos_row, slot_row, tile_col, tile_row,
    p1, p1t, p2, p2t,
    zkv_ss, zkv_rs, zq_ss, zq_rs, zm_ss, zm_rs,
    pkv_ss, pkv_rs, pq_ss, pq_rs, pm_ss, pm_rs,
    h_ss, hl_rs, hr_rs, po_ss, po_rs, zo_ss, zo_rs, win_s, pw_ss, pw_rs, zw_ss, zw_rs,
):
    seq, head = lax.axis_index("seq"), lax.axis_index("head")
    z, y = lax.div(seq, 4), lax.rem(seq, 4)
    x, core = lax.div(head, 2), lax.rem(head, 2)
    me = 2 * (4 * x + y + lax.rem(x, 2) * (3 - 2 * y)) + core

    def layer(j):
        return lax.rem(z + j, LAYERS)

    def peer(j):
        return lax.rem(me + j, OWNERS)

    def at_layer(zz):
        return device(zz, x, y, core)

    def at_owner(o):
        px, py, pc = place(o)
        return device(z, px, py, pc)

    barrier = pltpu.get_barrier_semaphore()

    @pl.loop(1, LAYERS)
    def _(j):
        pl.semaphore_signal(barrier, inc=1, device_id=at_layer(layer(j)), device_id_type=MESH)

    @pl.loop(1, OWNERS)
    def _(j):
        pl.semaphore_signal(barrier, inc=1, device_id=at_owner(peer(j)), device_id_type=MESH)

    pl.semaphore_wait(barrier, LAYERS - 1 + OWNERS - 1)

    def remote(src, dst, ss, rs, dev):
        pltpu.make_async_remote_copy(
            src_ref=src, dst_ref=dst, send_sem=ss, recv_sem=rs, device_id=dev, device_id_type=MESH
        ).start()

    my_rows = pl.ds(pl.multiple_of(z * ROWS, ROWS), ROWS)

    def z_send(src, h, dst, lanes, ss, rs):
        def columns(zz):
            return pl.ds(pl.multiple_of((zz * HEADS_HERE + h) * HEAD_DIM, HEAD_DIM), HEAD_DIM)

        for j in ORDER:
            zz = layer(j)
            remote(src.at[:, columns(zz)], dst.at[h, my_rows, lanes], ss, rs, at_layer(zz))
        pltpu.make_async_copy(src.at[:, columns(z)], dst.at[h, my_rows, lanes], rs).start()

    def z_send_kv(h):
        z_send(k_ref, h, zkv, pl.ds(0, HEAD_DIM), zkv_ss.at[h], zkv_rs.at[h])
        z_send(v_ref, h, zkv, pl.ds(HEAD_DIM, HEAD_DIM), zkv_ss.at[h], zkv_rs.at[h])

    def z_send_q(h):
        z_send(q_ref, h, zq, pl.ds(0, HEAD_DIM), zq_ss.at[h], zq_rs.at[h])

    my_share = pl.ds(pl.multiple_of(me * SHARE, SHARE), SHARE)

    def share(o):
        return pl.ds(pl.multiple_of(o * SHARE, SHARE), SHARE)

    def permute_send(table, src, stage, dst, ss, rs, owners=8):
        def store(i, rows, value):
            stage[rows, :] = value

            @pl.loop(0, owners)
            def _(j):
                o = i * owners + lax.rem(me + 1 + j, owners)

                @pl.when(o != me)
                def _():
                    remote(stage.at[share(o)], dst.at[my_share], ss, rs, at_owner(o))

                @pl.when(o == me)
                def _():
                    pltpu.make_async_copy(stage.at[my_share], dst.at[my_share], rs).start()

        permute(table, src, store, block=owners * SHARE, first=lax.div(me, owners))

    def permute(table, src, store, block=512, depth=256, first=0):
        @pl.loop(0, TOK_DEV // block)
        def _(step):
            i = lax.rem(step + first, TOK_DEV // block)
            rows = pl.ds(pl.multiple_of(i * block, block), block)
            total = None
            for k in range(0, TOK_DEV, depth):
                term = jnp.dot(
                    table[rows, k : k + depth],
                    src[k : k + depth, :],
                    preferred_element_type=jnp.float32,
                )
                total = term if total is None else total + term
            store(i, rows, total.astype(jnp.bfloat16))

    def into(ref):
        def store(i, rows, value):
            ref[rows, :] = value

        return store

    for j in ORDER:
        zz = layer(j)
        remote(slots_ref, zmeta.at[z], zm_ss, zm_rs, at_layer(zz))
        remote(windows_ref, zwin.at[z], zw_ss, zw_rs, at_layer(zz))
    pltpu.make_async_copy(slots_ref, zmeta.at[z], zm_rs).start()
    pltpu.make_async_copy(windows_ref, zwin.at[z], zw_rs).start()
    z_send_kv(0)
    z_send_q(0)
    z_send_kv(1)
    z_send_q(1)
    z_send_kv(2)
    z_send_q(2)

    bulk_wait(zmeta, zm_rs)

    @pl.loop(0, LAYERS)
    def _(s):
        wide = jnp.broadcast_to(zmeta[s].astype(jnp.float32), (ROWS, ROWS))
        diag = iota((ROWS, ROWS), 0) == iota((ROWS, ROWS), 1)
        col = jnp.sum(jnp.where(diag, wide, 0.0), axis=1, keepdims=True)
        rank = jnp.sum(jnp.where(wide < col, 1.0, 0.0), axis=1, keepdims=True)
        owner = jnp.floor((col + 0.5) * (1.0 / TOK_DEV))
        pos = owner * (SHARE - 6.0) + rank + (6 * s).astype(jnp.float32)
        rows = pl.ds(pl.multiple_of(s * ROWS, ROWS), ROWS)
        pos_col[rows, :] = jnp.broadcast_to(pos, (ROWS, 128))
        slot_col[rows, :] = jnp.broadcast_to(col, (ROWS, 128))

    def to_row(col_ref, row_ref):
        for b in range(TOK_DEV // 128):
            block = col_ref[b * 128 : (b + 1) * 128, :]
            diag = iota((128, 128), 0) == iota((128, 128), 1)
            row_ref[:, b * 128 : (b + 1) * 128] = jnp.sum(
                jnp.where(diag, block, 0.0), axis=0, keepdims=True
            )

    to_row(pos_col, pos_row)
    to_row(slot_col, slot_row)

    def table_by_row(table, row_ref, sorted_ref):
        @pl.loop(0, TOK_DEV // 64)
        def _(b):
            rows = pl.ds(pl.multiple_of(b * 64, 64), 64)
            want = (iota((64, TOK_DEV), 0) + b * 64).astype(jnp.float32)
            hit = want == row_ref[...]
            table[rows, :] = jnp.where(hit, 1.0, 0.0).astype(jnp.bfloat16)
            if sorted_ref is not None:
                slot = jnp.sum(jnp.where(hit, slot_row[...], 0.0), axis=1, keepdims=True)
                sorted_ref[rows, :] = jnp.broadcast_to(slot, (64, 128))

    def table_by_col(table, col_ref):
        @pl.loop(0, TOK_DEV // 64)
        def _(b):
            rows = pl.ds(pl.multiple_of(b * 64, 64), 64)
            want = iota((64, TOK_DEV), 1).astype(jnp.float32)
            hit = want == col_ref[rows, 0:1]
            table[rows, :] = jnp.where(hit, 1.0, 0.0).astype(jnp.bfloat16)

    def window_of(o):
        return zwin.at[lax.div(o, 4)]

    window_row = pltpu.make_async_copy(awin.at[2 * lax.rem(me, 4)], win_smem, win_s)

    def send_slots():
        table_by_row(p1, pos_row, slot_col)
        bulk_wait(zwin, zw_rs)

        @pl.loop(0, OWNERS)
        def _(o):
            block = slot_col[share(o), :]
            diag = iota((SHARE, 128), 0) == iota((SHARE, 128), 1)
            smeta[o] = jnp.sum(jnp.where(diag, block, 0.0), axis=0, keepdims=True)

        @pl.loop(1, OWNERS)
        def _(j):
            o = peer(j)
            remote(smeta.at[o], ameta.at[me], pm_ss, pm_rs, at_owner(o))
            remote(window_of(o), awin.at[me], pw_ss, pw_rs, at_owner(o))

        pltpu.make_async_copy(smeta.at[me], ameta.at[me], pm_rs).start()
        pltpu.make_async_copy(window_of(me), awin.at[me], pw_rs).start()

    def take_slots():
        bulk_wait(ameta, pm_rs)
        bulk_wait(awin, pw_rs)
        window_row.start()

        @pl.loop(0, OWNERS)
        def _(o):
            wide = jnp.broadcast_to(ameta[o], (SHARE, 128))
            diag = iota((SHARE, 128), 0) == iota((SHARE, 128), 1)
            col = jnp.sum(jnp.where(diag, wide, 0.0), axis=1, keepdims=True)
            col = col - (me * TOK_DEV).astype(jnp.float32)
            tile_col[share(o), :] = jnp.broadcast_to(col, (SHARE, 128))

        to_row(tile_col, tile_row)
        table_by_row(p2, tile_row, None)
        window_row.wait()

    def back_from_tiles():
        table_by_col(p2t, tile_col)

    def back_from_owners():
        table_by_col(p1t, pos_col)

    def sort_kv(h):
        bulk_wait(zkv.at[h], zkv_rs.at[h])
        permute_send(p1, zkv.at[h], skv.at[h], akv.at[h], pkv_ss.at[h], pkv_rs.at[h])

    def sort_q(h):
        bulk_wait(zq.at[h], zq_rs.at[h])
        permute_send(p1, zq.at[h], sq.at[h], aq.at[h], pq_ss.at[h], pq_rs.at[h])

    not_first, not_last = me > 0, me < OWNERS - 1

    def halo_copies(h):
        to_right = pltpu.make_async_remote_copy(
            src_ref=ekv.at[h, pl.ds(REACH + 1, REACH)],
            dst_ref=ekv.at[h, pl.ds(0, REACH)],
            send_sem=h_ss.at[0, h],
            recv_sem=hl_rs.at[h],
            device_id=at_owner(lax.rem(me + 1, OWNERS)),
            device_id_type=MESH,
        )
        to_left = pltpu.make_async_remote_copy(
            src_ref=ekv.at[h, pl.ds(REACH, REACH)],
            dst_ref=ekv.at[h, pl.ds(REACH + TILE_DEV, REACH)],
            send_sem=h_ss.at[1, h],
            recv_sem=hr_rs.at[h],
            device_id=at_owner(lax.rem(me + OWNERS - 1, OWNERS)),
            device_id_type=MESH,
        )
        return to_right, to_left

    def tile_kv(h):
        bulk_wait(akv.at[h], pkv_rs.at[h])

        def store(t, rows, value):
            ekv[h, REACH + t] = value

        permute(p2, akv.at[h], store, block=TILE)
        to_right, to_left = halo_copies(h)

        @pl.when(not_last)
        def _():
            to_right.start()

        @pl.when(not_first)
        def _():
            to_left.start()

    def halo_wait(h):
        to_right, to_left = halo_copies(h)

        @pl.when(not_first)
        def _():
            to_right.wait_recv()

        @pl.when(not_last)
        def _():
            to_left.wait_recv()

    factor = HEAD_DIM**-0.5 * LOG2E

    def tile_q(h):
        bulk_wait(aq.at[h], pq_rs.at[h])
        permute(p2, aq.at[h], into(tq.at[h]))

    def attend(h):
        halo_wait(h)

        @pl.loop(0, EXT_TILES)
        def _(e):
            ekw[e] = ekv[h, e]

        @pl.loop(0, TILE_DEV)
        def _(t):
            starts, biases = [], []
            for w in range(WIN):
                tile = win_smem[t, w]
                starts.append(lax.clamp(0, tile - (me * TILE_DEV - REACH), EXT_TILES - 1))
                biases.append(jnp.where(iota((1, TILE), 1) < valid_ref[tile], 0.0, FAR))
            real = valid_ref[me * TILE_DEV + t]
            rows = pl.ds(pl.multiple_of(t * TILE, TILE), TILE)
            query = tq[h, rows, :]
            scores = []
            for w in range(WIN):
                keys = ekw[starts[w], :, 0:HEAD_DIM]
                scores.append(
                    lax.dot_general(
                        query, keys, (((1,), (1,)), ((), ())), preferred_element_type=jnp.float32
                    )
                    + biases[w]
                )
            top = functools.reduce(
                jnp.maximum, [jnp.max(s, axis=1, keepdims=True) for s in scores]
            )
            weights = [jnp.exp2((s - top) * factor) for s in scores]
            total = functools.reduce(
                jnp.add, [jnp.sum(p, axis=1, keepdims=True) for p in weights]
            )
            mixed = None
            for w in range(WIN):
                values = ekw[starts[w], :, HEAD_DIM : 2 * HEAD_DIM]
                term = jnp.dot(
                    weights[w].astype(jnp.bfloat16), values, preferred_element_type=jnp.float32
                )
                mixed = term if mixed is None else mixed + term
            mixed = mixed / total
            keep = iota((TILE, 1), 0) < real
            ot[rows, :] = jnp.where(keep, mixed, 0.0).astype(jnp.bfloat16)

    def send_back(h):
        permute_send(p2t, ot, oa.at[h], ox.at[h], po_ss.at[h], po_rs.at[h])

    def unsort(h):
        bulk_wait(ox.at[h], po_rs.at[h])
        permute(p1t, ox.at[h], into(orr.at[h]))

    def give_back(h):
        columns = pl.ds(pl.multiple_of((z * HEADS_HERE + h) * HEAD_DIM, HEAD_DIM), HEAD_DIM)
        for j in ORDER:
            zz = layer(j)
            rows = pl.ds(pl.multiple_of(zz * ROWS, ROWS), ROWS)
            remote(orr.at[h, rows], out_ref.at[:, columns], zo_ss.at[h], zo_rs.at[h], at_layer(zz))
        pltpu.make_async_copy(orr.at[h, my_rows], out_ref.at[:, columns], zo_rs.at[h]).start()

    def unsort_give_back(h):
        bulk_wait(ox.at[h], po_rs.at[h])
        columns = pl.ds(pl.multiple_of((z * HEADS_HERE + h) * HEAD_DIM, HEAD_DIM), HEAD_DIM)

        def store(i, rows, value):
            orr[h, rows, :] = value
            for j in range(2):
                zz = i * 2 + j
                part = pl.ds(pl.multiple_of(zz * ROWS, ROWS), ROWS)

                @pl.when(zz != z)
                def _():
                    remote(
                        orr.at[h, part], out_ref.at[:, columns], zo_ss.at[h], zo_rs.at[h], at_layer(zz)
                    )

                @pl.when(zz == z)
                def _():
                    pltpu.make_async_copy(
                        orr.at[h, my_rows], out_ref.at[:, columns], zo_rs.at[h]
                    ).start()

        permute(p1t, ox.at[h], store, block=2 * ROWS, first=lax.div(layer(4), 2))

    send_slots()
    take_slots()
    sort_kv(0)
    back_from_tiles()
    back_from_owners()
    sort_q(0)
    tile_kv(0)
    tile_q(0)
    sort_kv(1)
    attend(0)
    send_back(0)
    sort_q(1)
    tile_kv(1)
    tile_q(1)
    unsort(0)
    sort_kv(2)
    attend(1)
    sort_q(2)
    give_back(0)
    tile_kv(2)
    tile_q(2)
    send_back(1)
    attend(2)
    send_back(2)
    unsort_give_back(1)
    unsort_give_back(2)

    bulk_wait(zmeta.at[pl.ds(0, LAYERS - 1)], zm_ss)
    bulk_wait(zwin.at[pl.ds(0, LAYERS - 1)], zw_ss)
    bulk_wait(smeta.at[pl.ds(0, OWNERS - 1)], pm_ss)
    bulk_wait(awin.at[pl.ds(0, OWNERS - 1)], pw_ss)
    z_sent = pl.ds(0, (LAYERS - 1) * ROWS)
    plane_sent = pl.ds(0, (OWNERS - 1) * SHARE)
    for h in range(HEADS_HERE):
        bulk_wait(zkv.at[h, z_sent], zkv_ss.at[h])
        bulk_wait(zq.at[h, z_sent], zq_ss.at[h])
        bulk_wait(skv.at[h, plane_sent], pkv_ss.at[h])
        bulk_wait(sq.at[h, plane_sent], pq_ss.at[h])
        bulk_wait(oa.at[h, plane_sent], po_ss.at[h])
        bulk_wait(orr.at[h, z_sent], zo_ss.at[h])
        to_right, to_left = halo_copies(h)

        @pl.when(not_last)
        def _():
            to_right.wait_send()

        @pl.when(not_first)
        def _():
            to_left.wait_send()

        bulk_wait(out_ref.at[:, pl.ds(0, LAYERS * HEAD_DIM)], zo_rs.at[h])


def body(query, key, value, raster_to_tile, window_list, valid_count):
    heads, bf16, dma = HEADS_HERE, jnp.bfloat16, pltpu.SemaphoreType.DMA
    vmem = pltpu.VMEM
    kv, one = 2 * HEAD_DIM, HEAD_DIM
    scratch = [
        vmem((heads, TOK_DEV, kv), bf16),
        vmem((heads, TOK_DEV, one), bf16),
        vmem((LAYERS, 1, ROWS), jnp.int32),
        vmem((LAYERS, TILE_DEV, WIN), jnp.int32),
        vmem((heads, TOK_DEV, kv), bf16),
        vmem((heads, TOK_DEV, one), bf16),
        vmem((heads, TOK_DEV, kv), bf16),
        vmem((heads, TOK_DEV, one), bf16),
        vmem((heads, EXT_TILES, TILE, kv), bf16),
        vmem((EXT_TILES, TILE, kv), bf16),
        vmem((heads, TOK_DEV, one), bf16),
        vmem((TOK_DEV, one), bf16),
        vmem((heads, TOK_DEV, one), bf16),
        vmem((heads, TOK_DEV, one), bf16),
        vmem((heads, TOK_DEV, one), bf16),
        vmem((OWNERS, 1, 128), jnp.float32),
        vmem((OWNERS, 1, 128), jnp.float32),
        vmem((OWNERS, TILE_DEV, WIN), jnp.int32),
        pltpu.SMEM((TILE_DEV, WIN), jnp.int32),
        vmem((TOK_DEV, 128), jnp.float32),
        vmem((TOK_DEV, 128), jnp.float32),
        vmem((1, TOK_DEV), jnp.float32),
        vmem((1, TOK_DEV), jnp.float32),
        vmem((TOK_DEV, 128), jnp.float32),
        vmem((1, TOK_DEV), jnp.float32),
        vmem((TOK_DEV, TOK_DEV), bf16),
        vmem((TOK_DEV, TOK_DEV), bf16),
        vmem((TOK_DEV, TOK_DEV), bf16),
        vmem((TOK_DEV, TOK_DEV), bf16),
        dma((heads,)), dma((heads,)), dma((heads,)), dma((heads,)), dma, dma,
        dma((heads,)), dma((heads,)), dma((heads,)), dma((heads,)), dma, dma,
        dma((2, heads)), dma((heads,)), dma((heads,)),
        dma((heads,)), dma((heads,)), dma((heads,)), dma((heads,)), dma, dma, dma, dma, dma,
    ]
    anywhere = pl.BlockSpec(memory_space=pl.ANY)
    return pl.pallas_call(
        kernel,
        out_shape=jax.ShapeDtypeStruct(query.shape, query.dtype),
        in_specs=[
            pl.BlockSpec(memory_space=pltpu.SMEM),
            anywhere,
            anywhere,
            anywhere,
            pl.BlockSpec(memory_space=vmem),
            pl.BlockSpec(memory_space=vmem),
        ],
        out_specs=anywhere,
        scratch_shapes=scratch,
        compiler_params=pltpu.CompilerParams(
            collective_id=0, has_side_effects=True, vmem_limit_bytes=58 * 2**20
        ),
    )(valid_count, query, key, value, raster_to_tile.reshape(1, ROWS), window_list)


def solution(mesh):
    placed = (
        P(("seq", "head"), None),
        P(("seq", "head"), None),
        P(("seq", "head"), None),
        P(("seq", "head")),
        P("seq", None),
        P(),
    )
    return jax.shard_map(
        body, mesh=mesh, in_specs=placed, out_specs=P(("seq", "head"), None), check_vma=False
    )
```
